512 devices in a mesh: fsdp: 64 (over z, x, core), ep: 8 (over y).
Axes of the slice: x: 4, y: 8, z: 8, core: 2. Of those that a mesh axis runs over, the one named last changes fastest.
Arguments:
- trainer_rows: bfloat16 [8, 8, 7680, 1024], P('ep', None, 'fsdp'), may hold values from -0.0625 to 0.0625
- row_counts: int32 [8, 8, 64], replicated, may hold values from 1 to 120, 7168 in all within a row
- rollout_map: int32 [8, 8], replicated, may hold values from 0 to 7, as said below
Outputs:
- codes: bfloat16 [8, 64, 7168, 128], P('ep', 'fsdp')
- block_scales: float32 [8, 64, 56], P('ep', 'fsdp')
The draws below stay inside these ranges and needn't reach their ends.
Inputs may be any that keep to these rules, and one draw needn't show every extreme that they name: For each k the entries rollout_map[k, g] over g are a permutation of the rollout devices; each trainer group sends exactly 1 of its experts to each rollout device. `row_counts`: the counts of one expert over the shards sum to 7168; in every expert some shard holds 120 rows.
All inputs are finite; a program needn't handle non-finite values. Where the reference program divides by a largest or mean magnitude, that divisor is 1e-20 or more.
Results may differ from the reference program's by a relative error of at most 0.001.
Values may be sent and summed in bfloat16 or wider, within the bound.
A program may use at most 64 MiB of HBM per device.

```python
import math
import jax
import jax.numpy as jnp
import numpy as np
from jax import lax

H = 7168
F = 1024
BLOCK = 128
EXP_LOC = 8
CAP = 120
COLBLK = 8
PAIR = 1
N_FSDP = 64
N_EP = 8


def draw_rollout_map(key, part):
    key = jax.random.fold_in(key, 11)
    first_key, second_key, third_key = jax.random.split(key, 3)
    group_shift = jax.random.permutation(first_key, N_EP)
    relabel = jax.random.permutation(second_key, N_EP)
    base_turns = (jnp.arange(EXP_LOC, dtype=jnp.int32) % N_EP).astype(jnp.int32)
    turn = jax.random.permutation(third_key, base_turns)
    return relabel[(group_shift[None, :] + turn[:, None]) % N_EP].astype(jnp.int32)


def block_levels(key, extent, cuts, least, top_value):
    def one(axis_at, blocks):
        draws = jax.random.uniform(jax.random.fold_in(jax.random.fold_in(key, 6), axis_at), (blocks,), jnp.float32, least / len(cuts), top_value / len(cuts))
        return jnp.repeat(jnp.exp(draws), extent[axis_at] // blocks).reshape((-1,) + (1,) * (len(extent) - axis_at - 1))

    gain = one(*cuts[0])
    for cut in cuts[1:]:
        gain = gain * one(*cut)
    return gain


def profile(amount, total, bound, slope):
    loads = [(1 << 20) // math.isqrt(rank ** slope) + 1 for rank in range(2, amount + 1)]
    rest, holding = total - bound - (amount - 1), [1] * (amount - 1)
    while rest > 0:
        free = [i for i in range(amount - 1) if holding[i] < bound]
        pool, remaining = sum([loads[i] for i in free]), rest
        for i in free:
            extra = min(bound - holding[i], max(1, remaining * loads[i] // pool), rest)
            holding[i] = holding[i] + extra
            rest = rest - extra
    return np.array([bound] + holding)


def ragged_sizes(own_key, count, total, limit, skew):
    if count == 2:
        one = jax.random.randint(own_key, (), max(1, total - limit), min(limit, total - 1) + 1)
        return jnp.stack([one, total - one])
    lengths = jnp.asarray(profile(count, total, limit, skew), jnp.int32)
    pairs = (count - 1) // 2
    giver, receiver = lengths[1:1 + 2 * pairs:2], lengths[2:2 + 2 * pairs:2]
    room = jnp.minimum(giver - 1, limit - receiver)
    moved = jax.random.randint(jax.random.fold_in(own_key, 1), (pairs,), 0, 1 << 20) % (room + 1)
    lengths = lengths.at[1:1 + 2 * pairs:2].set(giver - moved).at[2:2 + 2 * pairs:2].set(receiver + moved)
    return lengths[jax.random.permutation(jax.random.fold_in(own_key, 2), count)]


def scatter_about(own_key, shape, deviation, reach, cuts=(), kind=jnp.bfloat16):
    gain = block_levels(own_key, shape, cuts, -0.22, 0.18) if cuts else 1.0
    values = jax.random.normal(own_key, shape, jnp.float32) * deviation * gain
    return jnp.minimum(jnp.maximum(values, -reach), reach).astype(kind)


def setup_inputs(seed: int = 0) -> dict:
    key_of = jax.random.split(jax.random.key(seed), 4)
    trainer_rows = scatter_about(key_of[0], (N_EP, EXP_LOC, N_FSDP * CAP, F), H ** -0.5, 0.0625, ((0, 8), (2, 64)))
    row_counts = jax.vmap(lambda own: ragged_sizes(own, N_FSDP, H, CAP, 2))(jax.random.split(key_of[1], N_EP * EXP_LOC)).reshape((N_EP, EXP_LOC, N_FSDP)).astype(jnp.int32)
    rollout_map = draw_rollout_map(jax.random.fold_in(key_of[3], 71), 0)
    return {"trainer_rows": trainer_rows, "row_counts": row_counts, "rollout_map": rollout_map}


EPSILON = 1e-6
CODE_RANGE = 448.0


def order_ranks(rollout_map):
    per_group = rollout_map.shape[0]
    position = jnp.arange(per_group, dtype=jnp.int32)
    earlier = position[:, None] < position[None, :]
    same = rollout_map[:, None, :] == rollout_map[None, :, :]
    return jnp.sum((same & earlier[:, :, None]).astype(jnp.int32), axis=0).astype(jnp.int32)


def gather_rows(buffer, counts, buffer_rows):
    ends = jnp.cumsum(counts).astype(jnp.int32)
    height = jnp.arange(H, dtype=jnp.int32)
    passed = (ends[None, :] <= height[:, None]).astype(jnp.int32)
    index = (height + jnp.sum(passed * (buffer_rows - counts)[None, :], axis=1)).astype(jnp.int32)
    return jnp.take(buffer, index, axis=0)


def quantize(slab):
    values = slab.astype(jnp.float32).reshape(H // BLOCK, BLOCK, BLOCK)
    denom = jnp.max(jnp.abs(values), axis=(1, 2)) + EPSILON
    codes = (values / denom[:, None, None]).reshape(H, BLOCK).astype(jnp.bfloat16)
    return codes, denom / CODE_RANGE


def reference(trainer_rows, row_counts, rollout_map):
    ranks = order_ranks(rollout_map)
    position = jnp.arange(EXP_LOC, dtype=jnp.int32)

    def one_slot(item):
        target = item // EXP_LOC
        slot_id = item % EXP_LOC
        source = slot_id // PAIR
        within = slot_id % PAIR
        hit = (rollout_map[:, source] == target) & (ranks[:, source] == within)
        expert_at = jnp.sum(jnp.where(hit, position, 0)).astype(jnp.int32)
        rows = gather_rows(trainer_rows[source, expert_at], row_counts[source, expert_at], CAP)
        slabs = rows.reshape(H, COLBLK, BLOCK).transpose(1, 0, 2)
        return jax.vmap(quantize)(slabs)

    codes, scales = lax.map(one_slot, jnp.arange(N_EP * EXP_LOC, dtype=jnp.int32))
    codes = codes.reshape(N_EP, EXP_LOC * COLBLK, H, BLOCK)
    scales = scales.reshape(N_EP, EXP_LOC * COLBLK, H // BLOCK)
    return codes, scales
```

```python
import functools

import jax
import jax.numpy as jnp
from jax import lax
from jax.experimental import pallas as pl
from jax.experimental.pallas import tpu as pltpu
from jax.sharding import PartitionSpec as P

BLOCK = 128
EPSILON = 1e-06
CODE_RANGE = 448.0
LAG = 2
MESH = pl.DeviceIdType.MESH


def chunk_order(nx):
    order = [0, 2, 1, 3] if nx == 4 else list(range(nx))
    return [(dx, 0) for dx in order] + [(dx, 1) for dx in order[1:] + order[:1]]


def exchange_kernel(ny, nx, lag, map_ref, counts_ref, rows_ref, out_ref, send, relay, shift, ssem, s2sem, rsem, fsem):
    nxc = 2 * nx
    order = chunk_order(nx)
    cap = rows_ref.shape[1]
    f = lax.axis_index("fsdp")
    y = lax.axis_index("ep")
    z, xc = f // nxc, f % nxc
    x, core = xc // 2, xc % 2
    home = z == y

    barrier = pltpu.get_barrier_semaphore()

    def greet_plane(n, carry):
        to_xc, to_y = n // ny, n % ny

        @pl.when(jnp.logical_not((to_xc == xc) & (to_y == y)))
        def _():
            pl.semaphore_signal(barrier, inc=1, device_id=(z * nxc + to_xc, to_y), device_id_type=MESH)

        return carry

    def greet_column(n, carry):
        @pl.when(n != z)
        def _():
            pl.semaphore_signal(barrier, inc=1, device_id=(n * nxc + xc, y), device_id_type=MESH)

        return carry

    lax.fori_loop(0, nxc * ny, greet_plane, 0)
    lax.fori_loop(0, ny, greet_column, 0)

    mine = counts_ref[y].astype(jnp.float32)
    before = lax.broadcasted_iota(jnp.int32, mine.shape, 1) < f
    start = jnp.sum(jnp.where(before, mine, 0.0), axis=1, keepdims=True)
    start = start - cap * jnp.floor((start + 0.5) * (1.0 / cap))
    shift[...] = jnp.broadcast_to(start, shift.shape)
    gap = (
        lax.broadcasted_iota(jnp.int32, (cap, cap), 0) - lax.broadcasted_iota(jnp.int32, (cap, cap), 1)
    ).astype(jnp.float32)

    def offset(i):
        back = ny - 1 - i
        return ((back + 1) // 2) * (1 - 2 * ((back + 1) % 2)) + ny

    def tile(q, i):
        dx, dc = order[q]
        to_xc = ((x + (1 - 2 * core) * dx + nx) % nx) * 2 + (core + dc) % 2
        to_y = (y + offset(i)) % ny
        expert = 0
        for k in range(rows_ref.shape[0]):
            expert = jnp.where(map_ref[k, y] == to_y, k, expert)
        turn = shift[pl.ds(expert, 1), :][:, :cap]
        picker = ((gap == turn) | (gap == turn - cap)).astype(jnp.bfloat16)
        rows = rows_ref[expert, :, pl.ds(pl.multiple_of(to_xc * BLOCK, BLOCK), BLOCK)]
        turned = jnp.dot(picker, rows, preferred_element_type=jnp.float32)
        send[q * ny + i] = turned.astype(jnp.bfloat16)
        return to_xc, to_y

    def first_leg(q, i, to_xc, to_y):
        slot = q * ny + i
        own = (to_y == y) & (to_xc == xc)
        source = send.at[slot]

        @pl.when(jnp.logical_not(own) & jnp.logical_not(home))
        def _():
            pltpu.make_async_remote_copy(
                src_ref=source, dst_ref=relay.at[slot], send_sem=ssem, recv_sem=rsem.at[slot],
                device_id=(z * nxc + to_xc, to_y), device_id_type=MESH,
            ).start()

        @pl.when(jnp.logical_not(own) & home)
        def _():
            pltpu.make_async_remote_copy(
                src_ref=source, dst_ref=out_ref.at[f], send_sem=ssem, recv_sem=fsem,
                device_id=(z * nxc + to_xc, to_y), device_id_type=MESH,
            ).start()

        if order[q] == (0, 0):

            @pl.when(own & jnp.logical_not(home))
            def _():
                pltpu.make_async_remote_copy(
                    src_ref=source, dst_ref=out_ref.at[f], send_sem=ssem, recv_sem=fsem,
                    device_id=(y * nxc + xc, y), device_id_type=MESH,
                ).start()

            @pl.when(own & home)
            def _():
                pltpu.make_async_copy(source, out_ref.at[f], fsem).start()

    def second_leg(q, i):
        dx, dc = order[q]
        slot = q * ny + i
        from_y = (y - offset(i) + 2 * ny) % ny
        from_core = (core + dc) % 2
        from_xc = ((x - (1 - 2 * from_core) * dx + nx) % nx) * 2 + from_core
        moves = from_y != z
        if order[q] == (0, 0):
            moves = moves & (from_y != y)

        @pl.when(moves)
        def _():
            pltpu.make_async_copy(relay.at[slot], relay.at[slot], rsem.at[slot]).wait()
            pltpu.make_async_remote_copy(
                src_ref=relay.at[slot], dst_ref=out_ref.at[z * nxc + from_xc], send_sem=s2sem, recv_sem=fsem,
                device_id=(from_y * nxc + xc, y), device_id_type=MESH,
            ).start()

    chunks = len(order)
    for q in range(chunks + lag):
        if q < chunks:

            def push(i, carry):
                to_xc, to_y = tile(q, i)
                if q == 0:

                    @pl.when(i == 0)
                    def _():
                        pl.semaphore_wait(barrier, nxc * ny - 1 + ny - 1)

                first_leg(q, i, to_xc, to_y)
                return carry

            lax.fori_loop(0, ny, push, 0)
        if q >= lag:

            def pass_on(i, carry):
                second_leg(q - lag, i)
                return carry

            lax.fori_loop(0, ny, pass_on, 0)

    pltpu.make_async_copy(out_ref, out_ref, fsem).wait()
    total = nxc * ny

    @pl.when(home)
    def _():
        sent = send.at[pl.ds(0, total - 1)]
        pltpu.make_async_copy(sent, sent, ssem).wait()
        passed = relay.at[pl.ds(0, total - nxc)]
        pltpu.make_async_copy(passed, passed, s2sem).wait()

    @pl.when(jnp.logical_not(home))
    def _():
        pltpu.make_async_copy(send, send, ssem).wait()
        passed = relay.at[pl.ds(0, total - nxc - 1)]
        pltpu.make_async_copy(passed, passed, s2sem).wait()


def exchange(rows, row_counts, rollout_map, ny, nz, nx, lag=LAG, cid=0, name="exchange"):
    experts, cap, width = rows.shape
    tiles = (2 * nx * ny, cap, BLOCK)
    return pl.pallas_call(
        functools.partial(exchange_kernel, ny, nx, lag),
        name=name,
        out_shape=jax.ShapeDtypeStruct(tiles, jnp.bfloat16),
        in_specs=[
            pl.BlockSpec(memory_space=pltpu.SMEM),
            pl.BlockSpec(memory_space=pltpu.VMEM),
            pl.BlockSpec(memory_space=pltpu.VMEM),
        ],
        out_specs=pl.BlockSpec(memory_space=pl.ANY),
        scratch_shapes=[
            pltpu.VMEM(tiles, jnp.bfloat16),
            pltpu.VMEM(tiles, jnp.bfloat16),
            pltpu.VMEM((experts, 128), jnp.float32),
            pltpu.SemaphoreType.DMA,
            pltpu.SemaphoreType.DMA,
            pltpu.SemaphoreType.DMA((tiles[0],)),
            pltpu.SemaphoreType.DMA,
        ],
        compiler_params=pltpu.CompilerParams(
            collective_id=cid, has_side_effects=True, vmem_limit_bytes=32 << 20
        ),
    )(rollout_map, row_counts, rows)


def settle_kernel(
    nxc, parts, map_ref, counts_ref, tiles_ref, codes_ref, scales_ref, held, flat, most, codes, in_sem, out_sem
):
    shards, cap, _ = tiles_ref.shape
    blocks = most.shape[0]
    f = lax.axis_index("fsdp")
    y = lax.axis_index("ep")
    group = f // nxc
    expert = 0
    for k in range(map_ref.shape[0]):
        expert = jnp.where(map_ref[k, group] == y, k, expert)

    step = shards // parts

    def fetch(p):
        rows = pl.ds(p * step, step)
        return pltpu.make_async_copy(tiles_ref.at[rows], held.at[rows], in_sem.at[p])

    for p in range(parts):
        fetch(p).start()
    row = lax.broadcasted_iota(jnp.int32, (cap, BLOCK), 0)

    def place(n, carry):
        page, start, current = carry
        count = counts_ref[group, expert, n]
        here = held[n].astype(jnp.float32)
        current = jnp.where(row >= start, here, current)
        flat[pl.ds(pl.multiple_of(page * cap, 8), cap), :] = current
        start = start + count
        spill = start >= cap
        current = jnp.where(spill, here, current)
        return page + jnp.where(spill, 1, 0), start - jnp.where(spill, cap, 0), current

    carry = (jnp.int32(0), jnp.int32(0), jnp.zeros((cap, BLOCK), jnp.float32))
    for p in range(parts):
        fetch(p).wait()
        carry = lax.fori_loop(p * step, (p + 1) * step, place, carry)
    page, _, current = carry
    flat[pl.ds(pl.multiple_of(page * cap, 8), cap), :] = current

    def largest(b, carry):
        block = flat[pl.ds(pl.multiple_of(b * BLOCK, BLOCK), BLOCK), :]
        most[pl.ds(b, 1), :] = jnp.max(jnp.abs(block), axis=0, keepdims=True)
        return carry

    lax.fori_loop(0, blocks, largest, 0, unroll=4)
    denom = jnp.max(most[...], axis=1, keepdims=True) + EPSILON
    wide = jnp.broadcast_to(denom, most.shape)
    at = lax.broadcasted_iota(jnp.int32, wide.shape, 0)
    lane = lax.broadcasted_iota(jnp.int32, wide.shape, 1)
    line = jnp.sum(jnp.where(at == lane, wide, 0.0), axis=0, keepdims=True)
    scales_ref[0] = (line / CODE_RANGE)[:, :blocks]
    most[...] = 1.0 / wide

    def divide(b, carry):
        rows = pl.ds(pl.multiple_of(b * BLOCK, BLOCK), BLOCK)
        codes[rows, :] = (flat[rows, :] * most[pl.ds(b, 1), :]).astype(jnp.bfloat16)
        return carry

    share = blocks // parts

    def deliver(p):
        rows = pl.ds(p * share * BLOCK, share * BLOCK)
        return pltpu.make_async_copy(codes.at[rows], codes_ref.at[0, 0, rows], out_sem.at[p])

    for p in range(parts):
        lax.fori_loop(p * share, (p + 1) * share, divide, 0)
        deliver(p).start()
    for p in range(parts):
        deliver(p).wait()


def settle(tiles, row_counts, rollout_map, nxc, height, parts):
    shards, cap, _ = tiles.shape
    blocks = height // BLOCK
    pages = height // cap + 2
    return pl.pallas_call(
        functools.partial(settle_kernel, nxc, parts),
        name="settle",
        out_shape=(
            jax.ShapeDtypeStruct((1, 1, height, BLOCK), jnp.bfloat16),
            jax.ShapeDtypeStruct((1, 1, blocks), jnp.float32),
        ),
        in_specs=[
            pl.BlockSpec(memory_space=pltpu.SMEM),
            pl.BlockSpec(memory_space=pltpu.SMEM),
            pl.BlockSpec(memory_space=pl.ANY),
        ],
        out_specs=(pl.BlockSpec(memory_space=pl.ANY), pl.BlockSpec(memory_space=pltpu.VMEM)),
        scratch_shapes=[
            pltpu.VMEM(tiles.shape, jnp.bfloat16),
            pltpu.VMEM((pages * cap, BLOCK), jnp.float32),
            pltpu.VMEM((blocks, BLOCK), jnp.float32),
            pltpu.VMEM((height, BLOCK), jnp.bfloat16),
            pltpu.SemaphoreType.DMA((parts,)),
            pltpu.SemaphoreType.DMA((parts,)),
        ],
        compiler_params=pltpu.CompilerParams(vmem_limit_bytes=32 << 20),
    )(rollout_map, row_counts, tiles)


def on_device(height, trainer_rows, row_counts, rollout_map):
    ny = lax.axis_size("ep")
    nxc = trainer_rows.shape[-1] // BLOCK
    nz = lax.axis_size("fsdp") // nxc
    tiles = exchange(trainer_rows[0], row_counts, rollout_map, ny, nz, nxc // 2)
    parts = 8 if height % (8 * BLOCK) == 0 else 1
    return settle(tiles, row_counts, rollout_map, nxc, height, parts)


def solution(mesh, height=7168):
    placed = (P("ep", None, "fsdp", None), P(), P())
    return jax.shard_map(
        functools.partial(on_device, height),
        mesh=mesh,
        in_specs=placed,
        out_specs=(P("ep", "fsdp", None, None), P("ep", "fsdp", None)),
        check_vma=False,
    )
```

```python
import functools

import jax
import jax.numpy as jnp
from jax import lax
from jax.experimental import pallas as pl
from jax.experimental.pallas import tpu as pltpu
from jax.sharding import PartitionSpec as P

BLOCK = 128
EPSILON = 1e-06
CODE_RANGE = 448.0
LAG = 2
REST = 2
MESH = pl.DeviceIdType.MESH


def chunk_order(nx):
    order = [0, 2, 1, 3] if nx == 4 else list(range(nx))
    return [(dx, 0) for dx in order] + [(dx, 1) for dx in order[1:] + order[:1]]


def exchange_kernel(
    ny, nx, back, lag, rest, map_hbm, counts_hbm, rows_hbm, flat,
    map_ref, counts_ref, rows_ref, send, relay, held, shift, bounds, picker, in_sem, ssem, s2sem, rsem, fsem,
):
    nxc = 2 * nx
    order = chunk_order(nx)
    chunks = len(order)
    experts, cap, _ = rows_ref.shape
    f = lax.axis_index("fsdp")
    y = lax.axis_index("ep")
    z, xc = f // nxc, f % nxc
    x, core = xc // 2, xc % 2
    home = z == y

    fetches = [
        pltpu.make_async_copy(source, target, in_sem.at[n])
        for n, (source, target) in enumerate(
            ((map_hbm, map_ref), (counts_hbm, counts_ref), (rows_hbm.at[0], rows_ref))
        )
    ]
    for fetch in fetches:
        fetch.start()

    barrier = pltpu.get_barrier_semaphore()

    def greet_plane(n, carry):
        to_xc, to_y = n // ny, n % ny

        @pl.when(jnp.logical_not((to_xc == xc) & (to_y == y)))
        def _():
            pl.semaphore_signal(barrier, inc=1, device_id=(z * nxc + to_xc, to_y), device_id_type=MESH)

        return carry

    def greet_column(n, carry):
        @pl.when(n != z)
        def _():
            pl.semaphore_signal(barrier, inc=1, device_id=(n * nxc + xc, y), device_id_type=MESH)

        return carry

    lax.fori_loop(0, nxc * ny, greet_plane, 0)
    lax.fori_loop(0, ny, greet_column, 0)

    def offset(i):
        return ((i + 1) // 2) * (1 - 2 * ((i + 1) % 2)) + ny

    fetches[0].wait()
    fetches[1].wait()
    mine = counts_ref[y].astype(jnp.float32)
    before = lax.broadcasted_iota(jnp.int32, mine.shape, 1) < f
    start = jnp.sum(jnp.where(before, mine, 0.0), axis=1, keepdims=True)
    start = start - cap * jnp.floor((start + 0.5) * (1.0 / cap))
    shift[...] = jnp.broadcast_to(start, shift.shape)
    gap = (
        lax.broadcasted_iota(jnp.int32, (cap, cap), 0) - lax.broadcasted_iota(jnp.int32, (cap, cap), 1)
    ).astype(jnp.float32)
    chosen = []
    for i in range(ny):
        expert = 0
        for k in range(experts):
            expert = jnp.where(map_ref[k, y] == (y + offset(i)) % ny, k, expert)
        chosen.append(expert)
        turn = shift[pl.ds(expert, 1), :][:, :cap]
        picker[i] = ((gap == turn) | (gap == turn - cap)).astype(jnp.bfloat16)
    fetches[2].wait()

    def column(q):
        dx, dc = order[q]
        return ((x + (1 - 2 * core) * dx + nx) % nx) * 2 + (core + dc) % 2

    def source_column(q):
        dx, dc = order[q]
        from_core = (core + dc) % 2
        return ((x - (1 - 2 * from_core) * dx + nx) % nx) * 2 + from_core

    def turn_rows(q):
        lanes = pl.ds(pl.multiple_of(column(q) * BLOCK, BLOCK), BLOCK)
        for i in range(ny):
            turned = jnp.dot(picker[i], rows_ref[chosen[i], :, lanes], preferred_element_type=jnp.float32)
            send[q * ny + i] = turned.astype(jnp.bfloat16)

    def first_leg(q, i):
        slot = q * ny + i
        to_xc, to_y = column(q), (y + offset(i)) % ny
        own = (to_y == y) & (to_xc == xc)
        source = send.at[slot]
        landing = held.at[q * ny + z]

        @pl.when(jnp.logical_not(own) & jnp.logical_not(home))
        def _():
            pltpu.make_async_remote_copy(
                src_ref=source, dst_ref=relay.at[slot], send_sem=ssem, recv_sem=rsem.at[slot],
                device_id=(z * nxc + to_xc, to_y), device_id_type=MESH,
            ).start()

        @pl.when(jnp.logical_not(own) & home)
        def _():
            pltpu.make_async_remote_copy(
                src_ref=source, dst_ref=landing, send_sem=ssem, recv_sem=fsem.at[q],
                device_id=(z * nxc + to_xc, to_y), device_id_type=MESH,
            ).start()

        if order[q] == (0, 0):

            @pl.when(own & jnp.logical_not(home))
            def _():
                pltpu.make_async_remote_copy(
                    src_ref=source, dst_ref=landing, send_sem=ssem, recv_sem=fsem.at[q],
                    device_id=(y * nxc + xc, y), device_id_type=MESH,
                ).start()

            @pl.when(own & home)
            def _():
                pltpu.make_async_copy(source, landing, fsem.at[q]).start()

    def second_leg(q, i):
        slot = q * ny + i
        from_y = (y - offset(i) + 2 * ny) % ny
        moves = from_y != z
        if order[q] == (0, 0):
            moves = moves & (from_y != y)

        @pl.when(moves)
        def _():
            pltpu.make_async_copy(relay.at[slot], relay.at[slot], rsem.at[slot]).wait()
            pltpu.make_async_remote_copy(
                src_ref=relay.at[slot], dst_ref=held.at[q * ny + z], send_sem=s2sem, recv_sem=fsem.at[q],
                device_id=(from_y * nxc + xc, y), device_id_type=MESH,
            ).start()

    row = lax.broadcasted_iota(jnp.int32, (cap, BLOCK), 0).astype(jnp.float32)

    def find_bounds():
        expert = 0
        for k in range(experts):
            expert = jnp.where(map_ref[k, z] == y, k, expert)
        shards = counts_ref.shape[2]
        counts = jnp.broadcast_to(counts_ref[z, pl.ds(expert, 1), :].astype(jnp.float32), (shards, shards))
        at = lax.broadcasted_iota(jnp.int32, counts.shape, 0)
        other = lax.broadcasted_iota(jnp.int32, counts.shape, 1)
        for n, kept in enumerate((other < at, other <= at)):
            ends = jnp.sum(jnp.where(kept, counts, 0.0), axis=1, keepdims=True)
            bounds[n] = jnp.broadcast_to(ends, bounds.shape[1:])

    def place(q, from_z):
        shard = from_z * nxc + source_column(q)
        here = held[q * ny + from_z].astype(jnp.float32)
        base = (shard * cap).astype(jnp.float32)
        first = bounds[0, pl.ds(shard, 1), :] - base
        last = bounds[1, pl.ds(shard, 1), :] - base
        for d in range(back + 1):
            rows = pl.ds(pl.multiple_of((shard + back - d) * cap, 8), cap)
            inside = (row >= first + d * cap) & (row < last + d * cap)
            flat[rows, :] = jnp.where(inside, here, flat[rows, :])

    for q in range(chunks + lag + rest):
        if q < chunks:
            turn_rows(q)
            if q == 0:
                pl.semaphore_wait(barrier, nxc * ny - 1 + ny - 1)

            def push(i, carry):
                first_leg(q, i)
                return carry

            lax.fori_loop(0, ny, push, 0)
        if q == 0:
            find_bounds()
        if lag <= q < chunks + lag:

            def pass_on(i, carry):
                second_leg(q - lag, i)
                return carry

            lax.fori_loop(0, ny, pass_on, 0)
        if q >= lag + rest:
            done = q - lag - rest
            landed = held.at[pl.ds(done * ny, ny)]
            pltpu.make_async_copy(landed, landed, fsem.at[done]).wait()

            def place_one(from_z, carry):
                place(done, from_z)
                return carry

            lax.fori_loop(0, ny, place_one, 0)

    total = nxc * ny

    @pl.when(home)
    def _():
        sent = send.at[pl.ds(0, total - 1)]
        pltpu.make_async_copy(sent, sent, ssem).wait()
        passed = relay.at[pl.ds(0, total - nxc)]
        pltpu.make_async_copy(passed, passed, s2sem).wait()

    @pl.when(jnp.logical_not(home))
    def _():
        pltpu.make_async_copy(send, send, ssem).wait()
        passed = relay.at[pl.ds(0, total - nxc - 1)]
        pltpu.make_async_copy(passed, passed, s2sem).wait()


def pages_back(shards, cap, height):
    return -(-(shards * cap - height) // cap)


def exchange(rows, row_counts, rollout_map, height, ny, nx, lag=LAG, rest=REST, cid=0, name="exchange"):
    _, experts, cap, width = rows.shape
    shards = row_counts.shape[2]
    total = 2 * nx * ny
    back = pages_back(shards, cap, height)
    tiles = pltpu.VMEM((total, cap, BLOCK), jnp.bfloat16)
    return pl.pallas_call(
        functools.partial(exchange_kernel, ny, nx, back, lag, rest),
        name=name,
        out_shape=jax.ShapeDtypeStruct(((shards + back) * cap, BLOCK), jnp.float32),
        in_specs=[pl.BlockSpec(memory_space=pltpu.HBM)] * 3,
        out_specs=pl.BlockSpec(memory_space=pltpu.VMEM),
        scratch_shapes=[
            pltpu.SMEM(rollout_map.shape, jnp.int32),
            pltpu.VMEM(row_counts.shape, jnp.int32),
            pltpu.VMEM(rows.shape[1:], jnp.bfloat16),
            tiles,
            tiles,
            tiles,
            pltpu.VMEM((experts, BLOCK), jnp.float32),
            pltpu.VMEM((2, shards, BLOCK), jnp.float32),
            pltpu.VMEM((ny, cap, cap), jnp.bfloat16),
            pltpu.SemaphoreType.DMA((3,)),
            pltpu.SemaphoreType.DMA,
            pltpu.SemaphoreType.DMA,
            pltpu.SemaphoreType.DMA((total,)),
            pltpu.SemaphoreType.DMA((2 * nx,)),
        ],
        compiler_params=pltpu.CompilerParams(
            collective_id=cid, has_side_effects=True, vmem_limit_bytes=32 << 20
        ),
    )(*[pltpu.with_memory_space_constraint(array, pltpu.HBM) for array in (rollout_map, row_counts, rows)])


def settle_kernel(skip, parts, flat, codes_ref, scales_ref, most, codes, out_sem):
    blocks = most.shape[0]

    def rows_of(b):
        return flat[pl.ds(pl.multiple_of(skip + b * BLOCK, 8), BLOCK), :]

    share = blocks // parts

    def largest(b, carry):
        most[pl.ds(b, 1), :] = jnp.max(jnp.abs(rows_of(b)), axis=0, keepdims=True)
        return carry

    lax.fori_loop(0, blocks, largest, 0, unroll=share)
    denom = jnp.max(most[...], axis=1, keepdims=True) + EPSILON
    wide = jnp.broadcast_to(denom, most.shape)
    at = lax.broadcasted_iota(jnp.int32, wide.shape, 0)
    lane = lax.broadcasted_iota(jnp.int32, wide.shape, 1)
    line = jnp.sum(jnp.where(at == lane, wide, 0.0), axis=0, keepdims=True)
    scales_ref[0] = (line / CODE_RANGE)[:, :blocks]
    most[...] = 1.0 / wide

    def divide(b, carry):
        rows = pl.ds(pl.multiple_of(b * BLOCK, BLOCK), BLOCK)
        codes[rows, :] = (rows_of(b) * most[pl.ds(b, 1), :]).astype(jnp.bfloat16)
        return carry

    def deliver(p):
        rows = pl.ds(p * share * BLOCK, share * BLOCK)
        return pltpu.make_async_copy(codes.at[rows], codes_ref.at[0, 0, rows], out_sem.at[p])

    for p in range(parts):
        lax.fori_loop(p * share, (p + 1) * share, divide, 0, unroll=share)
        deliver(p).start()
    for p in range(parts):
        deliver(p).wait()


def settle(flat, skip, height, name="settle"):
    blocks = height // BLOCK
    parts = 8 if blocks % 8 == 0 else 1
    return pl.pallas_call(
        functools.partial(settle_kernel, skip, parts),
        name=name,
        out_shape=(
            jax.ShapeDtypeStruct((1, 1, height, BLOCK), jnp.bfloat16),
            jax.ShapeDtypeStruct((1, 1, blocks), jnp.float32),
        ),
        in_specs=[pl.BlockSpec(memory_space=pltpu.VMEM)],
        out_specs=(pl.BlockSpec(memory_space=pltpu.HBM), pl.BlockSpec(memory_space=pltpu.VMEM)),
        scratch_shapes=[
            pltpu.VMEM((blocks, BLOCK), jnp.float32),
            pltpu.VMEM((height, BLOCK), jnp.bfloat16),
            pltpu.SemaphoreType.DMA((parts,)),
        ],
        compiler_params=pltpu.CompilerParams(vmem_limit_bytes=32 << 20),
    )(flat)


def on_device(height, trainer_rows, row_counts, rollout_map):
    cap = trainer_rows.shape[2]
    ny = lax.axis_size("ep")
    nx = trainer_rows.shape[3] // BLOCK // 2
    flat = exchange(trainer_rows, row_counts, rollout_map, height, ny, nx)
    return settle(flat, pages_back(row_counts.shape[2], cap, height) * cap, height)


def solution(mesh, height=7168):
    placed = (P("ep", None, "fsdp", None), P(), P())
    return jax.shard_map(
        functools.partial(on_device, height),
        mesh=mesh,
        in_specs=placed,
        out_specs=(P("ep", "fsdp", None, None), P("ep", "fsdp", None)),
        check_vma=False,
    )
```

```python
import functools

import jax
import jax.numpy as jnp
from jax import lax
from jax.experimental import pallas as pl
from jax.experimental.pallas import tpu as pltpu
from jax.sharding import PartitionSpec as P

BLOCK = 128
EPSILON = 1e-06
CODE_RANGE = 448.0
LAG = 8
REST = 3
AHEAD = 4
MESH = pl.DeviceIdType.MESH


def chunk_order(nx):
    if nx == 4:
        return [(0, 0), (0, 1), (1, 0), (3, 0), (1, 1), (3, 1), (2, 0), (2, 1)]
    return [(0, 0), (0, 1)] + [(dx, dc) for dx in range(1, nx) for dc in (0, 1)]


def exchange_kernel(
    ny, nx, back, lag, rest, ahead, map_hbm, counts_hbm, rows_hbm, flat,
    map_ref, chosen, counts_ref, columns, send, middle, relay, held, shift, bounds, picker,
    in_sem, rows_sem, x_sem, y_sem, z_sem, x_here, y_here, here_sem,
):
    nxc = 2 * nx
    order = chunk_order(nx)
    chunks = len(order)
    experts, cap, _ = columns[0].shape
    f = lax.axis_index("fsdp")
    y = lax.axis_index("ep")
    z, xc = f // nxc, f % nxc
    x, core = xc // 2, xc % 2
    home = z == y

    def column(q):
        dx, dc = order[q]
        return ((x + (1 - 2 * core) * dx + nx) % nx) * 2 + (core + dc) % 2

    def source_column(q):
        dx, dc = order[q]
        from_core = (core + dc) % 2
        return ((x - (1 - 2 * from_core) * dx + nx) % nx) * 2 + from_core

    def fetch_column(q):
        lanes = pl.ds(pl.multiple_of(column(q) * BLOCK, BLOCK), BLOCK)
        return pltpu.make_async_copy(rows_hbm.at[0, :, :, lanes], columns[q], rows_sem.at[q])

    fetch_map = pltpu.make_async_copy(map_hbm, map_ref, in_sem.at[0])
    fetch_counts = pltpu.make_async_copy(counts_hbm, counts_ref, in_sem.at[1])
    fetch_map.start()
    fetch_counts.start()
    for q in range(chunks):
        fetch_column(q).start()

    barrier = pltpu.get_barrier_semaphore()
    for d in range(1, ny):
        pl.semaphore_signal(barrier, inc=1, device_id=(f, (y + d) % ny), device_id_type=MESH)
        pl.semaphore_signal(barrier, inc=1, device_id=((z + d) % ny * nxc + xc, y), device_id_type=MESH)
    for d in range(1, nxc):
        pl.semaphore_signal(barrier, inc=1, device_id=(z * nxc + (xc + d) % nxc, y), device_id_type=MESH)

    def paired(i):
        return ((i + 1) // 2) * (1 - 2 * ((i + 1) % 2)) + ny

    def offset(i):
        return paired(i) % ny

    fetch_map.wait()
    fetch_counts.wait()
    mine = counts_ref[y].astype(jnp.float32)
    before = lax.broadcasted_iota(jnp.int32, mine.shape, 1) < f
    start = jnp.sum(jnp.where(before, mine, 0.0), axis=1, keepdims=True)
    start = start - cap * jnp.floor((start + 0.5) * (1.0 / cap))
    shift[...] = jnp.broadcast_to(start, shift.shape)
    gap = (
        lax.broadcasted_iota(jnp.int32, (cap, cap), 0) - lax.broadcasted_iota(jnp.int32, (cap, cap), 1)
    ).astype(jnp.float32)

    def make_picker(step):
        expert = 0
        for k in range(experts):
            expert = jnp.where(map_ref[k, y] == (y + step) % ny, k, expert)
        chosen[step] = expert
        turn = shift[pl.ds(expert, 1), :][:, :cap]
        picker[step] = ((gap == turn) | (gap == turn - cap)).astype(jnp.bfloat16)

    def turn_rows(q, step):
        turned = jnp.dot(picker[step], columns[q][chosen[step]], preferred_element_type=jnp.float32)
        send[q * ny + step] = turned.astype(jnp.bfloat16)

    def along_x(q):
        tiles = pl.ds(q * ny, ny)
        pltpu.make_async_remote_copy(
            src_ref=send.at[tiles], dst_ref=middle.at[tiles], send_sem=x_sem, recv_sem=x_here.at[q],
            device_id=(z * nxc + column(q), y), device_id_type=MESH,
        ).start()

    def along_y(q, i):
        step = offset(i)
        slot = q * ny + step
        source = middle.at[slot] if q > 0 else send.at[slot]
        landing = held.at[q * ny + z]
        landed = here_sem.at[q * ny + z]
        stays = step == 0

        @pl.when(jnp.logical_not(stays) & jnp.logical_not(home))
        def _():
            pltpu.make_async_remote_copy(
                src_ref=source, dst_ref=relay.at[slot], send_sem=y_sem, recv_sem=y_here.at[slot],
                device_id=(f, (y + step) % ny), device_id_type=MESH,
            ).start()

        @pl.when(jnp.logical_not(stays) & home)
        def _():
            pltpu.make_async_remote_copy(
                src_ref=source, dst_ref=landing, send_sem=y_sem, recv_sem=landed,
                device_id=(f, (y + step) % ny), device_id_type=MESH,
            ).start()

        @pl.when(stays & jnp.logical_not(home))
        def _():
            pltpu.make_async_remote_copy(
                src_ref=source, dst_ref=landing, send_sem=y_sem, recv_sem=landed,
                device_id=(y * nxc + xc, y), device_id_type=MESH,
            ).start()

        @pl.when(stays & home)
        def _():
            pltpu.make_async_copy(source, landing, landed).start()

    def along_z(q, i):
        step = offset(i)
        slot = q * ny + step
        from_y = (y - step + ny) % ny

        @pl.when((from_y != z) & (step != 0))
        def _():
            pltpu.make_async_copy(relay.at[slot], relay.at[slot], y_here.at[slot]).wait()
            pltpu.make_async_remote_copy(
                src_ref=relay.at[slot], dst_ref=held.at[q * ny + z], send_sem=z_sem,
                recv_sem=here_sem.at[q * ny + z], device_id=(from_y * nxc + xc, y), device_id_type=MESH,
            ).start()

    row = lax.broadcasted_iota(jnp.int32, (cap, BLOCK), 0).astype(jnp.float32)

    def find_bounds():
        expert = 0
        for k in range(experts):
            expert = jnp.where(map_ref[k, z] == y, k, expert)
        shards = counts_ref.shape[2]
        counts = jnp.broadcast_to(counts_ref[z, pl.ds(expert, 1), :].astype(jnp.float32), (shards, shards))
        at = lax.broadcasted_iota(jnp.int32, counts.shape, 0)
        other = lax.broadcasted_iota(jnp.int32, counts.shape, 1)
        for n, kept in enumerate((other < at, other <= at)):
            ends = jnp.sum(jnp.where(kept, counts, 0.0), axis=1, keepdims=True)
            bounds[n] = jnp.broadcast_to(ends, bounds.shape[1:])

    def place(q, i):
        from_z = (z + offset(i)) % ny
        slot = q * ny + from_z
        pltpu.make_async_copy(held.at[slot], held.at[slot], here_sem.at[slot]).wait()
        shard = from_z * nxc + source_column(q)
        here = held[slot].astype(jnp.float32)
        base = (shard * cap).astype(jnp.float32)
        first = bounds[0, pl.ds(shard, 1), :] - base
        last = bounds[1, pl.ds(shard, 1), :] - base
        for d in range(back + 1):
            rows = pl.ds(pl.multiple_of((shard + back - d) * cap, 8), cap)
            inside = (row >= first + d * cap) & (row < last + d * cap)
            flat[rows, :] = jnp.where(inside, here, flat[rows, :])

    fetch_column(0).wait()
    for i in range(ny):
        step = offset(i)
        make_picker(step)
        turn_rows(0, step)
        if i == 0:
            pl.semaphore_wait(barrier, 2 * (ny - 1) + nxc - 1)
        along_y(0, i)
    ahead = min(ahead, chunks - 1)
    for q in range(1, ahead + 1):
        fetch_column(q).wait()
        for step in range(ny):
            turn_rows(q, step)
        along_x(q)
    find_bounds()

    half = ny // 2
    for q in range(1, chunks + rest + 1):
        if q < chunks:
            tiles = middle.at[pl.ds(q * ny, ny)]
            pltpu.make_async_copy(tiles, tiles, x_here.at[q]).wait()
        if ahead + q < chunks:
            fetch_column(ahead + q).wait()
        for part in range(2):
            behind = (2 * q + part) * half - lag
            z_at, z_from = behind // ny, behind % ny

            def step_of(n, carry):
                i = part * half + n
                if q < chunks:
                    along_y(q, i)
                if ahead + q < chunks:
                    turn_rows(ahead + q, i)
                if 0 <= q - rest < chunks:
                    place(q - rest, i)
                if 0 <= z_at < chunks:
                    along_z(z_at, z_from + n)
                return carry

            lax.fori_loop(0, half, step_of, 0)
        if ahead + q < chunks:
            along_x(ahead + q)
    def drain(buffer, tiles, semaphore):
        if tiles == 0:
            return
        part = buffer.at[pl.ds(0, tiles)]
        pltpu.make_async_copy(part, part, semaphore).wait()

    drain(send, (chunks - 1) * ny, x_sem)

    @pl.when(home)
    def _():
        drain(send, chunks * (ny - 1), y_sem)
        drain(relay, chunks * (ny - 1), z_sem)

    @pl.when(jnp.logical_not(home))
    def _():
        drain(send, chunks * ny, y_sem)
        drain(relay, chunks * (ny - 2), z_sem)


def pages_back(shards, cap, height):
    return -(-(shards * cap - height) // cap)


def exchange(rows, row_counts, rollout_map, height, ny, nx, lag=LAG, rest=REST, ahead=AHEAD, cid=0, name="exchange"):
    _, experts, cap, width = rows.shape
    shards = row_counts.shape[2]
    total = 2 * nx * ny
    back = pages_back(shards, cap, height)
    tiles = pltpu.VMEM((total, cap, BLOCK), jnp.bfloat16)
    return pl.pallas_call(
        functools.partial(exchange_kernel, ny, nx, back, lag, rest, ahead),
        name=name,
        out_shape=jax.ShapeDtypeStruct(((shards + back) * cap, BLOCK), jnp.float32),
        in_specs=[pl.BlockSpec(memory_space=pltpu.HBM)] * 3,
        out_specs=pl.BlockSpec(memory_space=pltpu.VMEM),
        scratch_shapes=[
            pltpu.SMEM(rollout_map.shape, jnp.int32),
            pltpu.SMEM((ny,), jnp.int32),
            pltpu.VMEM(row_counts.shape, jnp.int32),
            [pltpu.VMEM((experts, cap, BLOCK), jnp.bfloat16)] * (2 * nx),
            tiles,
            tiles,
            tiles,
            tiles,
            pltpu.VMEM((experts, BLOCK), jnp.float32),
            pltpu.VMEM((2, shards, BLOCK), jnp.float32),
            pltpu.VMEM((ny, cap, cap), jnp.bfloat16),
            pltpu.SemaphoreType.DMA((2,)),
            pltpu.SemaphoreType.DMA((2 * nx,)),
            pltpu.SemaphoreType.DMA,
            pltpu.SemaphoreType.DMA,
            pltpu.SemaphoreType.DMA,
            pltpu.SemaphoreType.DMA((2 * nx,)),
            pltpu.SemaphoreType.DMA((total,)),
            pltpu.SemaphoreType.DMA((total,)),
        ],
        compiler_params=pltpu.CompilerParams(
            collective_id=cid, has_side_effects=True, vmem_limit_bytes=32 << 20
        ),
    )(*[pltpu.with_memory_space_constraint(array, pltpu.HBM) for array in (rollout_map, row_counts, rows)])


def settle_kernel(skip, parts, flat, codes_ref, scales_ref, most, codes, out_sem):
    blocks = most.shape[0]

    def rows_of(b):
        return flat[pl.ds(pl.multiple_of(skip + b * BLOCK, 8), BLOCK), :]

    share = blocks // parts

    def largest(b, carry):
        most[pl.ds(b, 1), :] = jnp.max(jnp.abs(rows_of(b)), axis=0, keepdims=True)
        return carry

    lax.fori_loop(0, blocks, largest, 0, unroll=share)
    denom = jnp.max(most[...], axis=1, keepdims=True) + EPSILON
    wide = jnp.broadcast_to(denom, most.shape)
    at = lax.broadcasted_iota(jnp.int32, wide.shape, 0)
    lane = lax.broadcasted_iota(jnp.int32, wide.shape, 1)
    line = jnp.sum(jnp.where(at == lane, wide, 0.0), axis=0, keepdims=True)
    scales_ref[0] = (line / CODE_RANGE)[:, :blocks]
    most[...] = 1.0 / wide

    def divide(b, carry):
        rows = pl.ds(pl.multiple_of(b * BLOCK, BLOCK), BLOCK)
        codes[rows, :] = (rows_of(b) * most[pl.ds(b, 1), :]).astype(jnp.bfloat16)
        return carry

    def deliver(p):
        rows = pl.ds(p * share * BLOCK, share * BLOCK)
        return pltpu.make_async_copy(codes.at[rows], codes_ref.at[0, 0, rows], out_sem.at[p])

    for p in range(parts):
        lax.fori_loop(p * share, (p + 1) * share, divide, 0, unroll=share)
        deliver(p).start()
    for p in range(parts):
        deliver(p).wait()


def settle(flat, skip, height, name="settle"):
    blocks = height // BLOCK
    parts = 8 if blocks % 8 == 0 else 1
    return pl.pallas_call(
        functools.partial(settle_kernel, skip, parts),
        name=name,
        out_shape=(
            jax.ShapeDtypeStruct((1, 1, height, BLOCK), jnp.bfloat16),
            jax.ShapeDtypeStruct((1, 1, blocks), jnp.float32),
        ),
        in_specs=[pl.BlockSpec(memory_space=pltpu.VMEM)],
        out_specs=(pl.BlockSpec(memory_space=pltpu.HBM), pl.BlockSpec(memory_space=pltpu.VMEM)),
        scratch_shapes=[
            pltpu.VMEM((blocks, BLOCK), jnp.float32),
            pltpu.VMEM((height, BLOCK), jnp.bfloat16),
            pltpu.SemaphoreType.DMA((parts,)),
        ],
        compiler_params=pltpu.CompilerParams(vmem_limit_bytes=32 << 20),
    )(flat)


def on_device(height, trainer_rows, row_counts, rollout_map):
    cap = trainer_rows.shape[2]
    ny = lax.axis_size("ep")
    nx = trainer_rows.shape[3] // BLOCK // 2
    flat = exchange(trainer_rows, row_counts, rollout_map, height, ny, nx)
    return settle(flat, pages_back(row_counts.shape[2], cap, height) * cap, height)


def solution(mesh, height=7168):
    placed = (P("ep", None, "fsdp", None), P(), P())
    return jax.shard_map(
        functools.partial(on_device, height),
        mesh=mesh,
        in_specs=placed,
        out_specs=(P("ep", "fsdp", None, None), P("ep", "fsdp", None)),
        check_vma=False,
    )
```

```python
import functools

import jax
import jax.numpy as jnp
from jax import lax
from jax.experimental import pallas as pl
from jax.experimental.pallas import tpu as pltpu
from jax.sharding import PartitionSpec as P

BLOCK = 128
EPSILON = 1e-06
CODE_RANGE = 448.0
LAG = 8
REST = 3
AHEAD = 4
MESH = pl.DeviceIdType.MESH


def chunk_order(nx):
    if nx == 4:
        return [(0, 0), (0, 1), (1, 0), (3, 0), (1, 1), (3, 1), (2, 0), (2, 1)]
    return [(0, 0), (0, 1)] + [(dx, dc) for dx in range(1, nx) for dc in (0, 1)]


def exchange_kernel(
    ny, nx, back, lag, rest, ahead, map_hbm, counts_hbm, rows_hbm, flat,
    map_ref, chosen, counts_ref, columns, send, middle, relay, held, shift, bounds, picker,
    in_sem, rows_sem, x_sem, y_sem, z_sem, x_here, y_here, here_sem,
):
    nxc = 2 * nx
    order = chunk_order(nx)
    chunks = len(order)
    experts, cap, _ = columns[0].shape
    f = lax.axis_index("fsdp")
    y = lax.axis_index("ep")
    z, xc = f // nxc, f % nxc
    x, core = xc // 2, xc % 2
    home = z == y

    def column(q):
        dx, dc = order[q]
        return ((x + (1 - 2 * core) * dx + nx) % nx) * 2 + (core + dc) % 2

    def source_column(q):
        dx, dc = order[q]
        from_core = (core + dc) % 2
        return ((x - (1 - 2 * from_core) * dx + nx) % nx) * 2 + from_core

    def fetch_column(q):
        lanes = pl.ds(pl.multiple_of(column(q) * BLOCK, BLOCK), BLOCK)
        return pltpu.make_async_copy(rows_hbm.at[0, :, :, lanes], columns[q], rows_sem.at[q])

    fetch_map = pltpu.make_async_copy(map_hbm, map_ref, in_sem.at[0])
    fetch_counts = pltpu.make_async_copy(counts_hbm, counts_ref, in_sem.at[1])
    fetch_map.start()
    fetch_counts.start()
    fetch_column(0).start()

    barrier = pltpu.get_barrier_semaphore()
    for d in range(1, ny):
        pl.semaphore_signal(barrier, inc=1, device_id=(f, (y + d) % ny), device_id_type=MESH)
        pl.semaphore_signal(barrier, inc=1, device_id=((z + d) % ny * nxc + xc, y), device_id_type=MESH)
    for d in range(1, nxc):
        pl.semaphore_signal(barrier, inc=1, device_id=(z * nxc + (xc + d) % nxc, y), device_id_type=MESH)

    for q in range(1, chunks):
        fetch_column(q).start()

    def paired(i):
        return ((i + 1) // 2) * (1 - 2 * ((i + 1) % 2)) + ny

    def offset(i):
        return paired(i) % ny

    fetch_map.wait()
    fetch_counts.wait()
    mine = counts_ref[y].astype(jnp.float32)
    before = lax.broadcasted_iota(jnp.int32, mine.shape, 1) < f
    start = jnp.sum(jnp.where(before, mine, 0.0), axis=1, keepdims=True)
    start = start - cap * jnp.floor((start + 0.5) * (1.0 / cap))
    shift[...] = jnp.broadcast_to(start, shift.shape)
    gap = (
        lax.broadcasted_iota(jnp.int32, (cap, cap), 0) - lax.broadcasted_iota(jnp.int32, (cap, cap), 1)
    ).astype(jnp.float32)

    def make_picker(step):
        expert = 0
        for k in range(experts):
            expert = jnp.where(map_ref[k, y] == (y + step) % ny, k, expert)
        chosen[step] = expert
        turn = shift[pl.ds(expert, 1), :][:, :cap]
        picker[step] = ((gap == turn) | (gap == turn - cap)).astype(jnp.bfloat16)

    def turn_rows(q, step):
        turned = jnp.dot(picker[step], columns[q][chosen[step]], preferred_element_type=jnp.float32)
        send[q * ny + step] = turned.astype(jnp.bfloat16)

    def along_x(q):
        tiles = pl.ds(q * ny, ny)
        pltpu.make_async_remote_copy(
            src_ref=send.at[tiles], dst_ref=middle.at[tiles], send_sem=x_sem, recv_sem=x_here.at[q],
            device_id=(z * nxc + column(q), y), device_id_type=MESH,
        ).start()

    def along_y(q, i):
        step = offset(i)
        slot = q * ny + step
        source = middle.at[slot] if q > 0 else send.at[slot]
        landing = held.at[q * ny + z]
        landed = here_sem.at[q * ny + z]
        stays = step == 0

        @pl.when(jnp.logical_not(stays) & jnp.logical_not(home))
        def _():
            pltpu.make_async_remote_copy(
                src_ref=source, dst_ref=relay.at[slot], send_sem=y_sem, recv_sem=y_here.at[slot],
                device_id=(f, (y + step) % ny), device_id_type=MESH,
            ).start()

        @pl.when(jnp.logical_not(stays) & home)
        def _():
            pltpu.make_async_remote_copy(
                src_ref=source, dst_ref=landing, send_sem=y_sem, recv_sem=landed,
                device_id=(f, (y + step) % ny), device_id_type=MESH,
            ).start()

        @pl.when(stays & jnp.logical_not(home))
        def _():
            pltpu.make_async_remote_copy(
                src_ref=source, dst_ref=landing, send_sem=y_sem, recv_sem=landed,
                device_id=(y * nxc + xc, y), device_id_type=MESH,
            ).start()

        @pl.when(stays & home)
        def _():
            pltpu.make_async_copy(source, landing, landed).start()

    def along_z(q, i):
        step = offset(i)
        slot = q * ny + step
        from_y = (y - step + ny) % ny

        @pl.when((from_y != z) & (step != 0))
        def _():
            pltpu.make_async_copy(relay.at[slot], relay.at[slot], y_here.at[slot]).wait()
            pltpu.make_async_remote_copy(
                src_ref=relay.at[slot], dst_ref=held.at[q * ny + z], send_sem=z_sem,
                recv_sem=here_sem.at[q * ny + z], device_id=(from_y * nxc + xc, y), device_id_type=MESH,
            ).start()

    row = lax.broadcasted_iota(jnp.int32, (cap, BLOCK), 0).astype(jnp.float32)

    def find_bounds():
        expert = 0
        for k in range(experts):
            expert = jnp.where(map_ref[k, z] == y, k, expert)
        shards = counts_ref.shape[2]
        counts = jnp.broadcast_to(counts_ref[z, pl.ds(expert, 1), :].astype(jnp.float32), (shards, shards))
        at = lax.broadcasted_iota(jnp.int32, counts.shape, 0)
        other = lax.broadcasted_iota(jnp.int32, counts.shape, 1)
        for n, kept in enumerate((other < at, other <= at)):
            ends = jnp.sum(jnp.where(kept, counts, 0.0), axis=1, keepdims=True)
            bounds[n] = jnp.broadcast_to(ends, bounds.shape[1:])

    def place(q, i):
        from_z = (z + offset(i)) % ny
        slot = q * ny + from_z
        pltpu.make_async_copy(held.at[slot], held.at[slot], here_sem.at[slot]).wait()
        shard = from_z * nxc + source_column(q)
        here = held[slot].astype(jnp.float32)
        base = (shard * cap).astype(jnp.float32)
        first = bounds[0, pl.ds(shard, 1), :] - base
        last = bounds[1, pl.ds(shard, 1), :] - base
        for d in range(back + 1):
            rows = pl.ds(pl.multiple_of((shard + back - d) * cap, 8), cap)
            inside = (row >= first + d * cap) & (row < last + d * cap)
            flat[rows, :] = jnp.where(inside, here, flat[rows, :])

    fetch_column(0).wait()
    for i in range(ny):
        step = offset(i)
        make_picker(step)
        turn_rows(0, step)
        if i == 0:
            pl.semaphore_wait(barrier, 2 * (ny - 1) + nxc - 1)
        along_y(0, i)
    ahead = min(ahead, chunks - 1)
    for q in range(1, ahead + 1):
        fetch_column(q).wait()
        for step in range(ny):
            turn_rows(q, step)
        along_x(q)
    find_bounds()

    half = ny // 2
    for q in range(1, chunks + rest + 1):
        if q < chunks:
            tiles = middle.at[pl.ds(q * ny, ny)]
            pltpu.make_async_copy(tiles, tiles, x_here.at[q]).wait()
        if ahead + q < chunks:
            fetch_column(ahead + q).wait()
        for part in range(2):
            behind = (2 * q + part) * half - lag
            z_at, z_from = behind // ny, behind % ny

            def step_of(n, carry):
                i = part * half + n
                if q < chunks:
                    along_y(q, i)
                if ahead + q < chunks:
                    turn_rows(ahead + q, i)
                if 0 <= q - rest < chunks:
                    place(q - rest, i)
                if 0 <= z_at < chunks:
                    along_z(z_at, z_from + n)
                return carry

            lax.fori_loop(0, half, step_of, 0)
        if ahead + q < chunks:
            along_x(ahead + q)
    def drain(buffer, tiles, semaphore):
        if tiles == 0:
            return
        part = buffer.at[pl.ds(0, tiles)]
        pltpu.make_async_copy(part, part, semaphore).wait()

    drain(send, (chunks - 1) * ny, x_sem)

    @pl.when(home)
    def _():
        drain(send, chunks * (ny - 1), y_sem)
        drain(relay, chunks * (ny - 1), z_sem)

    @pl.when(jnp.logical_not(home))
    def _():
        drain(send, chunks * ny, y_sem)
        drain(relay, chunks * (ny - 2), z_sem)


def pages_back(shards, cap, height):
    return -(-(shards * cap - height) // cap)


def exchange(rows, row_counts, rollout_map, height, ny, nx, lag=LAG, rest=REST, ahead=AHEAD, cid=0, name="exchange"):
    _, experts, cap, width = rows.shape
    shards = row_counts.shape[2]
    total = 2 * nx * ny
    back = pages_back(shards, cap, height)
    tiles = pltpu.VMEM((total, cap, BLOCK), jnp.bfloat16)
    return pl.pallas_call(
        functools.partial(exchange_kernel, ny, nx, back, lag, rest, ahead),
        name=name,
        out_shape=jax.ShapeDtypeStruct(((shards + back) * cap, BLOCK), jnp.float32),
        in_specs=[pl.BlockSpec(memory_space=pltpu.HBM)] * 3,
        out_specs=pl.BlockSpec(memory_space=pltpu.VMEM),
        scratch_shapes=[
            pltpu.SMEM(rollout_map.shape, jnp.int32),
            pltpu.SMEM((ny,), jnp.int32),
            pltpu.VMEM(row_counts.shape, jnp.int32),
            [pltpu.VMEM((experts, cap, BLOCK), jnp.bfloat16)] * (2 * nx),
            tiles,
            tiles,
            tiles,
            tiles,
            pltpu.VMEM((experts, BLOCK), jnp.float32),
            pltpu.VMEM((2, shards, BLOCK), jnp.float32),
            pltpu.VMEM((ny, cap, cap), jnp.bfloat16),
            pltpu.SemaphoreType.DMA((2,)),
            pltpu.SemaphoreType.DMA((2 * nx,)),
            pltpu.SemaphoreType.DMA,
            pltpu.SemaphoreType.DMA,
            pltpu.SemaphoreType.DMA,
            pltpu.SemaphoreType.DMA((2 * nx,)),
            pltpu.SemaphoreType.DMA((total,)),
            pltpu.SemaphoreType.DMA((total,)),
        ],
        compiler_params=pltpu.CompilerParams(
            collective_id=cid, has_side_effects=True, vmem_limit_bytes=32 << 20
        ),
    )(*[pltpu.with_memory_space_constraint(array, pltpu.HBM) for array in (rollout_map, row_counts, rows)])


def settle_kernel(skip, parts, flat, codes_ref, scales_ref, most, codes, out_sem):
    blocks = most.shape[0]

    def rows_of(b):
        return flat[pl.ds(pl.multiple_of(skip + b * BLOCK, 8), BLOCK), :]

    share = blocks // parts

    def largest(b, carry):
        most[pl.ds(b, 1), :] = jnp.max(jnp.abs(rows_of(b)), axis=0, keepdims=True)
        return carry

    lax.fori_loop(0, blocks, largest, 0, unroll=share)
    denom = jnp.max(most[...], axis=1, keepdims=True) + EPSILON
    wide = jnp.broadcast_to(denom, most.shape)
    at = lax.broadcasted_iota(jnp.int32, wide.shape, 0)
    lane = lax.broadcasted_iota(jnp.int32, wide.shape, 1)
    line = jnp.sum(jnp.where(at == lane, wide, 0.0), axis=0, keepdims=True)
    scales_ref[0] = (line / CODE_RANGE)[:, :blocks]
    most[...] = 1.0 / wide

    def divide(b, carry):
        rows = pl.ds(pl.multiple_of(b * BLOCK, BLOCK), BLOCK)
        codes[rows, :] = (rows_of(b) * most[pl.ds(b, 1), :]).astype(jnp.bfloat16)
        return carry

    def deliver(p):
        rows = pl.ds(p * share * BLOCK, share * BLOCK)
        return pltpu.make_async_copy(codes.at[rows], codes_ref.at[0, 0, rows], out_sem.at[p])

    for p in range(parts):
        lax.fori_loop(p * share, (p + 1) * share, divide, 0, unroll=share)
        deliver(p).start()
    for p in range(parts):
        deliver(p).wait()


def settle(flat, skip, height, name="settle"):
    blocks = height // BLOCK
    parts = 8 if blocks % 8 == 0 else 1
    return pl.pallas_call(
        functools.partial(settle_kernel, skip, parts),
        name=name,
        out_shape=(
            jax.ShapeDtypeStruct((1, 1, height, BLOCK), jnp.bfloat16),
            jax.ShapeDtypeStruct((1, 1, blocks), jnp.float32),
        ),
        in_specs=[pl.BlockSpec(memory_space=pltpu.VMEM)],
        out_specs=(pl.BlockSpec(memory_space=pltpu.HBM), pl.BlockSpec(memory_space=pltpu.VMEM)),
        scratch_shapes=[
            pltpu.VMEM((blocks, BLOCK), jnp.float32),
            pltpu.VMEM((height, BLOCK), jnp.bfloat16),
            pltpu.SemaphoreType.DMA((parts,)),
        ],
        compiler_params=pltpu.CompilerParams(vmem_limit_bytes=32 << 20),
    )(flat)


def on_device(height, trainer_rows, row_counts, rollout_map):
    cap = trainer_rows.shape[2]
    ny = lax.axis_size("ep")
    nx = trainer_rows.shape[3] // BLOCK // 2
    flat = exchange(trainer_rows, row_counts, rollout_map, height, ny, nx)
    return settle(flat, pages_back(row_counts.shape[2], cap, height) * cap, height)


def solution(mesh, height=7168):
    placed = (P("ep", None, "fsdp", None), P(), P())
    return jax.shard_map(
        functools.partial(on_device, height),
        mesh=mesh,
        in_specs=placed,
        out_specs=(P("ep", "fsdp", None, None), P("ep", "fsdp", None)),
        check_vma=False,
    )
```
